32 devices in a mesh: gx: 2 (over y), gy: 4 (over x, core), gz: 4 (over z).
Axes of the slice: x: 2, y: 2, z: 4, core: 2. Of those that a mesh axis runs over, the one named last changes fastest.
Arguments:
- iterate: float32 [16, 64, 512], P('gx', 'gy', 'gz'), may hold values from -6 to 6
- source: float32 [16, 64, 512], P('gx', 'gy', 'gz'), may hold values from -6 to 6
- permeability: float32 [16, 64, 512], P('gx', 'gy', 'gz'), may hold values from 0.1 to 10
- storage: float32 [16, 64, 512], P('gx', 'gy', 'gz'), may hold values from 0.01 to 0.1
Outputs:
- updated: float32 [16, 64, 512], P('gx', 'gy', 'gz')
The draws below stay inside these ranges and needn't reach their ends.
All inputs are finite; a program needn't handle non-finite values.
Results may differ from the reference program's by a relative error of at most 0.0003.
Values sent between devices are 32-bit elements; how exact they have to be, the bound alone decides.
A program may use at most 64 MiB of HBM per device.

```python
import math
import jax
import jax.numpy as jnp
from jax import lax

CX = 8
CY = 16
CZ = 128
MARGIN = 3
COARSEN = 8
NEWTON = 2
SWEEPS = 4
CSWEEPS = 6
NX = 16
NY = 64
NZ = 512
N_GX = 2
N_GY = 4
N_GZ = 4


def levels(own_key, extent, split, smallest, high):
    level = 1.0
    for position, blocks in split:
        steps = jax.random.uniform(jax.random.fold_in(jax.random.fold_in(own_key, 6), position), (blocks,), jnp.float32, smallest / len(split), high / len(split))
        level = level * jnp.repeat(jnp.exp(steps), extent[position] // blocks).reshape((-1,) + (1,) * (len(extent) - 1 - position))
    return level


def scatter_about(stream_key, extent, scale, reach, pieces=(), kind=jnp.bfloat16):
    entries = scale * jax.random.normal(stream_key, extent, jnp.float32)
    if pieces:
        entries = entries * levels(stream_key, extent, pieces, -0.22, 0.18)
    return jnp.clip(entries, -reach, reach).astype(kind)


def setup_inputs(seed: int = 0) -> dict:
    splits = jax.random.split(jax.random.key(seed), 5)
    iterate = scatter_about(splits[0], (NX, NY, NZ), 1.0, 6.0, ((0, 2), (1, 4), (2, 4)), jnp.float32)
    source = scatter_about(splits[1], (NX, NY, NZ), 1.0, 6.0, ((0, 2), (1, 4), (2, 4)), jnp.float32)
    permeability = jnp.clip(jnp.exp(math.log(10.0) - 4.6051702 * jax.random.uniform(splits[2], (NX, NY, NZ), jnp.float32) ** levels(splits[2], (NX, NY, NZ), ((0, 2), (1, 4), (2, 4)), -0.2, 0.2)), 0.1, 10.0)
    storage = jnp.clip(jnp.exp(math.log(0.1) - 2.3025851 * jax.random.uniform(splits[3], (NX, NY, NZ), jnp.float32) ** levels(splits[3], (NX, NY, NZ), ((0, 2), (1, 4), (2, 4)), -0.2, 0.2)), 0.01, 0.1)
    return dict(iterate=iterate, source=source, permeability=permeability, storage=storage)


def cut(array, axis, piece, rest):
    index = [rest, rest, rest]
    index[axis] = piece
    return array[tuple(index)]


def face_partitions(padded, coef_pad, inv):
    partition_list = []
    diffs = []
    for axis in range(3):
        upper = cut(padded, axis, slice(1, None), slice(1, -1))
        lower = cut(padded, axis, slice(0, -1), slice(1, -1))
        kupper = cut(coef_pad, axis, slice(1, None), slice(1, -1))
        klower = cut(coef_pad, axis, slice(0, -1), slice(1, -1))
        diff = upper - lower
        scaled = diff * inv
        coef = 0.5 * (kupper + klower) * (1.0 + scaled * scaled) ** -0.25 * (inv * inv)
        partition_list.append(coef)
        diffs.append(diff)
    flow_operator = 0.0
    partition_weight = 0.0
    for axis in range(3):
        flux = partition_list[axis] * diffs[axis]
        flow_operator = flow_operator + cut(flux, axis, slice(1, None), slice(None)) - cut(flux, axis, slice(0, -1), slice(None))
        partition_weight = partition_weight + cut(partition_list[axis], axis, slice(1, None), slice(None)) + cut(partition_list[axis], axis, slice(0, -1), slice(None))
    return partition_list, flow_operator, partition_weight


def neighbour(partition_list, delta_pad):
    total = 0.0
    for axis in range(3):
        total = total + cut(partition_list[axis], axis, slice(1, None), slice(None)) * cut(delta_pad, axis, slice(2, None), slice(1, -1))
        total = total + cut(partition_list[axis], axis, slice(0, -1), slice(None)) * cut(delta_pad, axis, slice(0, -2), slice(1, -1))
    return total


def local_subdomain_newton(value_padded, permeability_padded, reaction_term, right_hand_side):
    interior_region = value_padded[1:-1, 1:-1, 1:-1]
    for step in range(NEWTON):
        partition_list, flow_operator, partition_weight = face_partitions(value_padded, permeability_padded, 1.0)
        res = right_hand_side - reaction_term * interior_region + flow_operator
        diag = reaction_term + partition_weight
        delta = res / diag
        for sweep in range(SWEEPS - 1):
            delta = (res + neighbour(partition_list, jnp.pad(delta, 1))) / diag
        interior_region = interior_region + delta
        value_padded = value_padded.at[1:-1, 1:-1, 1:-1].set(interior_region)
    return interior_region


def restrict(field):
    a, b, c = field.shape
    grouped = field.reshape(a // COARSEN, COARSEN, b // COARSEN, COARSEN, c // COARSEN, COARSEN)
    return jnp.sum(grouped, axis=(1, 3, 5)) * (1.0 / COARSEN ** 3)


def prolong(field):
    a, b, c = field.shape
    spread = jnp.broadcast_to(field[:, None, :, None, :, None], (a, COARSEN, b, COARSEN, c, COARSEN))
    return spread.reshape(a * COARSEN, b * COARSEN, c * COARSEN)


def wrap_pad(field):
    return jnp.pad(field, 1, mode="wrap")


def reference(iterate, source, permeability, storage):
    width = MARGIN + 1
    upad = jnp.pad(iterate, width, mode="wrap")
    fpad = jnp.pad(source, width, mode="wrap")
    permeability_padded = jnp.pad(permeability, width, mode="wrap")
    cpad = jnp.pad(storage, width, mode="wrap")
    shape = (CX + 2 * width, CY + 2 * width, CZ + 2 * width)

    def one_block(idx):
        ix = idx // (N_GY * N_GZ)
        iy = (idx // N_GZ) % N_GY
        iz = idx % N_GZ
        start = (ix * CX, iy * CY, iz * CZ)
        start = tuple(jnp.asarray(s).astype(jnp.int32) for s in start)
        vblock = lax.dynamic_slice(upad, start, shape)
        kblock = lax.dynamic_slice(permeability_padded, start, shape)
        fblock = lax.dynamic_slice(fpad, start, shape)[1:-1, 1:-1, 1:-1]
        cblock = lax.dynamic_slice(cpad, start, shape)[1:-1, 1:-1, 1:-1]
        interior_region = local_subdomain_newton(vblock, kblock, cblock, fblock)
        return interior_region[MARGIN:-MARGIN, MARGIN:-MARGIN, MARGIN:-MARGIN]

    blocks = lax.map(one_block, jnp.arange(N_GX * N_GY * N_GZ, dtype=jnp.int32))
    combined = blocks.reshape(N_GX, N_GY, N_GZ, CX, CY, CZ).transpose(0, 3, 1, 4, 2, 5).reshape(NX, NY, NZ)
    partition_list, flow_operator, partition_weight = face_partitions(wrap_pad(combined), wrap_pad(permeability), 1.0)
    fine_res = source - storage * combined + flow_operator
    coarse_base = restrict(combined)
    coarse_res = restrict(fine_res)
    coarse_perm = restrict(permeability)
    coarse_store = restrict(storage)
    inv = 1.0 / COARSEN
    kcpad = wrap_pad(coarse_perm)
    partition_list, flow_operator, partition_weight = face_partitions(wrap_pad(coarse_base), kcpad, inv)
    coarse_rhs = coarse_store * coarse_base - flow_operator + coarse_res
    z = coarse_base
    for sweep in range(CSWEEPS):
        partition_list, flow_operator, partition_weight = face_partitions(wrap_pad(z), kcpad, inv)
        z = z + (coarse_rhs - coarse_store * z + flow_operator) / (coarse_store + partition_weight)
    return combined + prolong(z - coarse_base)
```

```python
import functools

import jax
import jax.numpy as jnp
from jax import lax
from jax.experimental import pallas as pl
from jax.experimental.pallas import tpu as pltpu
from jax.sharding import PartitionSpec as P

NEWTON = 2
SWEEPS = 4
CSWEEPS = 6
AXES = ("gx", "gy", "gz")
F32 = jnp.float32
ROWS = 152
FIRST = 8
LAST = 144
CHUNK = 16
ITER, SRC, PERM, STORE = 0, 1, 2, 3
ORDER = (ITER, PERM, SRC, STORE)


def g(d):
    y = d * d + 1.0
    r = lax.rsqrt(y)
    return lax.rsqrt(y * r)


def iota(shape, dim):
    return lax.broadcasted_iota(jnp.int32, shape, dim)


def roll(v, shift, axis):
    return pltpu.roll(v, shift % v.shape[axis], axis)


def y_up(tiles):
    rolled = [roll(v, -16, 1) for v in tiles]
    inside = iota(tiles[0].shape, 1) < 112
    return [jnp.where(inside, rolled[t], rolled[(t + 1) % 3]) for t in range(3)]


def y_down(tiles):
    rolled = [roll(v, 16, 1) for v in tiles]
    inside = iota(tiles[0].shape, 1) >= 16
    return [jnp.where(inside, rolled[t], rolled[(t - 1) % 3]) for t in range(3)]


def chunks():
    at = FIRST
    while at < LAST:
        size = min(CHUNK, LAST - at)
        yield at, size
        at += size


def newton(T, AX, AY, AZ, FZ, RES, RD, D):
    for it in range(NEWTON):
        for r, n in chunks():
            v = [T[ITER, t, r : r + n, :] for t in range(3)]
            k = [T[PERM, t, r : r + n, :] for t in range(3)]
            vy, ky = y_up(v), y_up(k)
            ay, fy, ax, fx = [], [], [], []
            for t in range(3):
                d = vy[t] - v[t]
                a = (0.5 * (ky[t] + k[t])) * g(d)
                AY[t, r : r + n, :] = a
                ay.append(a)
                fy.append(a * d)
                d = roll(v[t], -1, 1) - v[t]
                a = (0.5 * (roll(k[t], -1, 1) + k[t])) * g(d)
                AX[t, r : r + n, :] = a
                ax.append(a)
                fx.append(a * d)
            aym, fym = y_down(ay), y_down(fy)
            lane = iota((n, 128), 1)
            row = iota((n, 128), 0) + (r - FIRST)
            x, yl = lane % 16, lane // 16
            for t in range(3):
                d = T[ITER, t, r + 1 : r + n + 1, :] - v[t]
                az = (0.5 * (T[PERM, t, r + 1 : r + n + 1, :] + k[t])) * g(d)
                fz = az * d
                AZ[t, r : r + n, :] = az
                FZ[t, r : r + n, :] = fz
                azm = AZ[t, r - 1 : r + n - 1, :]
                fzm = FZ[t, r - 1 : r + n - 1, :]
                flow = (fz - fzm) + (fy[t] - fym[t]) + (fx[t] - roll(fx[t], 1, 1))
                weight = (az + azm) + (ay[t] + aym[t]) + (ax[t] + roll(ax[t], 1, 1))
                c = T[STORE, t, r : r + n, :]
                res = T[SRC, t, r : r + n, :] - c * v[t] + flow
                y = yl + 8 * t
                known = (x >= 1) & (x <= 14) & (y >= 1) & (y <= 22) & (row >= 1) & (row <= 134)
                rd = jnp.where(known, 1.0 / (c + weight), 0.0)
                RES[t, r : r + n, :] = res
                RD[t, r : r + n, :] = rd
                D[0, t, r : r + n, :] = res * rd
        for sweep in range(SWEEPS - 1):
            old, new = sweep % 2, (sweep + 1) % 2
            for r, n in chunks():
                d = [D[old, t, r : r + n, :] for t in range(3)]
                ay = [AY[t, r : r + n, :] for t in range(3)]
                up = y_up(d)
                down = y_down([ay[t] * d[t] for t in range(3)])
                for t in range(3):
                    ax = AX[t, r : r + n, :]
                    total = RES[t, r : r + n, :] + ay[t] * up[t] + down[t]
                    total += ax * roll(d[t], -1, 1) + roll(ax * d[t], 1, 1)
                    total += AZ[t, r : r + n, :] * D[old, t, r + 1 : r + n + 1, :]
                    total += AZ[t, r - 1 : r + n - 1, :] * D[old, t, r - 1 : r + n - 1, :]
                    delta = total * RD[t, r : r + n, :]
                    if sweep < SWEEPS - 2:
                        D[new, t, r : r + n, :] = delta
                    else:
                        T[ITER, t, r : r + n, :] = T[ITER, t, r : r + n, :] + delta


def coarse_flow(z, k, inv):
    n = len(z)
    flow, weight = [], []
    up = []
    for i in range(n):
        d = z[(i + 1) % n] - z[i]
        a = (0.5 * inv * inv * (k[(i + 1) % n] + k[i])) * g(d * inv)
        up.append((a, a * d))
    for i in range(n):
        a, f = up[i]
        am, fm = up[i - 1]
        w, fl = a + am, f - fm
        for axis in range(2):
            d = roll(z[i], -1, axis) - z[i]
            a = (0.5 * inv * inv * (roll(k[i], -1, axis) + k[i])) * g(d * inv)
            f = a * d
            w = w + (a + roll(a, 1, axis))
            fl = fl + (f - roll(f, 1, axis))
        flow.append(fl)
        weight.append(w)
    return flow, weight


def kernel(
    sizes, it_ref, src_ref, perm_ref, store_ref, out,
    I, XR, PA, T, ZS, ZR, AX, AY, AZ, FZ, RES, RD, D, Q, CB, XS, XF, YF, FS, ZF,
    GS, GZ, GM, GY, GV, GX, CR,
    lsem, xs_sem, xr_sem, ys_sem, yr_sem, zs_sem, zr_sem, fs_sem, fr_sem, gs_sem, gr_sem,
):
    nx, ny, nz = sizes
    size = dict(zip(AXES, sizes))
    me = {name: lax.axis_index(name) for name in AXES}

    def there(name, step):
        return {name: lax.rem(me[name] + (step + size[name]), size[name])}

    def send(src, dst, s, r, name, step):
        copy = pltpu.make_async_remote_copy(
            src_ref=src, dst_ref=dst, send_sem=s, recv_sem=r,
            device_id=there(name, step), device_id_type=pl.DeviceIdType.MESH,
        )
        copy.start()
        return copy

    barrier = pltpu.get_barrier_semaphore()
    for name in AXES:
        for step in range(1, size[name]):
            pl.semaphore_signal(
                barrier, inc=1, device_id=there(name, step), device_id_type=pl.DeviceIdType.MESH
            )
    local = {}
    for a, ref in enumerate((it_ref, src_ref, perm_ref, store_ref)):
        local[a] = pltpu.make_async_copy(ref, I.at[a], lsem.at[a])
        local[a].start()
    for buf in (T,):
        for a in range(4):
            for t in range(3):
                buf[a, t, 0:FIRST, :] = jnp.zeros((FIRST, 128), F32)
                buf[a, t, LAST:ROWS, :] = jnp.zeros((ROWS - LAST, 128), F32)
    for buf in (AZ, FZ):
        for t in range(3):
            buf[t, 0:FIRST, :] = jnp.zeros((FIRST, 128), F32)
    for b in range(2):
        for t in range(3):
            D[b, t, 0:FIRST, :] = jnp.zeros((FIRST, 128), F32)
            D[b, t, LAST:ROWS, :] = jnp.zeros((ROWS - LAST, 128), F32)
    for a in range(4):
        local[a].wait()
    pl.semaphore_wait(barrier, nx + ny + nz - 3)

    sent = []
    xcopy, ycopy, zcopy = {}, {}, {}
    for a in ORDER:
        hi = send(I.at[a, pl.ds(64, 64)], XR.at[a, 0], xs_sem.at[2 * a], xr_sem.at[2 * a], "gx", 1)
        lo = send(I.at[a, pl.ds(0, 64)], XR.at[a, 1], xs_sem.at[2 * a + 1], xr_sem.at[2 * a + 1], "gx", -1)
        xcopy[a] = (hi, lo)
        sent += [hi, lo]
    for a in ORDER:
        for x in range(8):
            PA[a, pl.ds(64 + 4 + x, 16, stride=16), :] = I[a, 16 * x : 16 * x + 16, :]
    for a in ORDER:
        for side in range(2):
            xcopy[a][side].wait_recv()
            for x in range(4):
                PA[a, pl.ds(64 + 12 * side + x, 16, stride=16), :] = XR[a, side, 16 * x : 16 * x + 16, :]
        hi = send(PA.at[a, pl.ds(256, 64)], PA.at[a, pl.ds(0, 64)], ys_sem.at[2 * a], yr_sem.at[2 * a], "gy", 1)
        lo = send(PA.at[a, pl.ds(64, 64)], PA.at[a, pl.ds(320, 64)], ys_sem.at[2 * a + 1], yr_sem.at[2 * a + 1], "gy", -1)
        ycopy[a] = (hi, lo)
        sent += [hi, lo]
    for p in range(2):
        for h in range(2):
            a = ORDER[2 * p + h]
            ycopy[a][0].wait_recv()
            ycopy[a][1].wait_recv()
            for t in range(3):
                m = PA[a, 128 * t : 128 * t + 128, :].T
                T[a, t, 12:140, :] = m
                ZS[p, 0, t, 4 * h : 4 * h + 4, :] = m[124:128, :]
                ZS[p, 1, t, 4 * h : 4 * h + 4, :] = m[0:4, :]
        hi = send(ZS.at[p, 0], ZR.at[p, 0], zs_sem.at[2 * p], zr_sem.at[2 * p], "gz", 1)
        lo = send(ZS.at[p, 1], ZR.at[p, 1], zs_sem.at[2 * p + 1], zr_sem.at[2 * p + 1], "gz", -1)
        zcopy[p] = (hi, lo)
        sent += [hi, lo]
    for p in range(2):
        zcopy[p][0].wait_recv()
        zcopy[p][1].wait_recv()
        for h in range(2):
            a = ORDER[2 * p + h]
            for t in range(3):
                T[a, t, 8:12, :] = ZR[p, 0, t, 4 * h : 4 * h + 4, :]
                T[a, t, 140:144, :] = ZR[p, 1, t, 4 * h : 4 * h + 4, :]

    newton(T, AX, AY, AZ, FZ, RES, RD, D)

    for t in range(3):
        Q[128 * t : 128 * t + 128, :] = T[ITER, t, 12:140, :].T
    lane = iota((8, 128), 1)
    pack_c = jnp.zeros((8, 128), F32)
    pack_k = jnp.zeros((8, 128), F32)
    for y in range(16):
        b = (y + 4) * 16 + 4
        c = Q[b : b + 8, :]
        CB[8 * y : 8 * y + 8, :] = c
        pack_c = jnp.where(lane // 2 == y, roll(c, 1 + 2 * y, 1), pack_c)
        pack_k = jnp.where(lane // 2 == y, roll(PA[PERM, b : b + 8, :], 1 + 2 * y, 1), pack_k)
    XS[0, :, :] = Q[pl.ds(64 + 11, 16, stride=16), :]
    XS[1, :, :] = Q[pl.ds(64 + 4, 16, stride=16), :]
    FS[0:8, :] = pack_c
    FS[8:16, :] = pack_k
    faces = [
        send(XS.at[0], XF.at[0], fs_sem.at[0], fr_sem.at[0], "gx", 1),
        send(XS.at[1], XF.at[1], fs_sem.at[1], fr_sem.at[1], "gx", -1),
        send(CB.at[pl.ds(120, 8)], YF.at[0], fs_sem.at[2], fr_sem.at[2], "gy", 1),
        send(CB.at[pl.ds(0, 8)], YF.at[1], fs_sem.at[3], fr_sem.at[3], "gy", -1),
        send(FS, ZF.at[0], fs_sem.at[4], fr_sem.at[4], "gz", 1),
        send(FS, ZF.at[1], fs_sem.at[5], fr_sem.at[5], "gz", -1),
    ]
    sent += faces
    for copy in faces:
        copy.wait_recv()
    Q[pl.ds(64 + 3, 16, stride=16), :] = XF[0, :, :]
    Q[pl.ds(64 + 12, 16, stride=16), :] = XF[1, :, :]
    Q[3 * 16 + 4 : 3 * 16 + 12, :] = YF[0, :, :]
    Q[20 * 16 + 4 : 20 * 16 + 12, :] = YF[1, :, :]

    sums = [[None, None] for _ in range(4)]

    def add(q, j, value):
        sums[q][j] = value if sums[q][j] is None else sums[q][j] + value

    zf = [ZF[0, 0:8, :], ZF[1, 0:8, :]]
    zk = [ZF[0, 8:16, :], ZF[1, 8:16, :]]
    for y in range(16):
        b = (y + 4) * 16 + 4
        c, k = Q[b : b + 8, :], PA[PERM, b : b + 8, :]
        near = [(Q[b + o : b + o + 8, :], PA[PERM, b + o : b + o + 8, :]) for o in (1, -1, 16, -16)]
        near.append(tuple(
            jnp.where(lane == 127, roll(far, 126 - 2 * y, 1), roll(own, -1, 1))
            for far, own in ((zf[1], c), (zk[1], k))
        ))
        near.append(tuple(
            jnp.where(lane == 0, roll(far, -2 * y, 1), roll(own, 1, 1))
            for far, own in ((zf[0], c), (zk[0], k))
        ))
        flow = 0.0
        for cn, kn in near:
            d = cn - c
            flow = flow + (0.5 * (k + kn)) * g(d) * d
        st = PA[STORE, b : b + 8, :]
        j = y // 8
        add(0, j, c)
        add(1, j, PA[SRC, b : b + 8, :] - st * c + flow)
        add(2, j, k)
        add(3, j, st)
    rows = [jnp.sum(sums[q][j], axis=0, keepdims=True) for q in range(4) for j in range(2)]
    mean = jnp.where(iota((128, 128), 0) // 8 == iota((128, 128), 1) % 16, 1.0 / 512, 0.0).astype(F32)
    tile = jnp.dot(
        jnp.concatenate(rows, axis=0), mean,
        precision=lax.Precision.HIGHEST, preferred_element_type=F32,
    )

    width = GM.shape[-1]

    def gather(src, buf, name, base):
        n = size[name]
        copies = [
            send(src, buf.at[me[name]], gs_sem.at[base + s - 1], gr_sem.at[base + s - 1], name, s)
            for s in range(1, n)
        ]
        buf[me[name]] = src[...]
        for copy in copies:
            copy.wait_recv()
        sent.extend(copies)

    GS[...] = tile
    gather(GS, GZ, "gz", 0)
    wlane = iota((8, width), 1)
    merged = None
    for z in range(nz):
        part = GZ[z]
        if width > 128:
            part = jnp.concatenate([part] * (width // 128), axis=1)
        merged = part if merged is None else jnp.where((wlane // 16) % nz == z, part, merged)
    GM[...] = merged
    gather(GM, GY, "gy", nz - 1)
    for y in range(ny):
        for q in range(4):
            GV[8 * q + 2 * y : 8 * q + 2 * y + 2, :] = GY[y, 2 * q : 2 * q + 2, :]
    gather(GV, GX, "gx", nz + ny - 2)

    base = [GX[i, 0:8, :] for i in range(nx)]
    cres = [GX[i, 8:16, :] for i in range(nx)]
    kc = [GX[i, 16:24, :] for i in range(nx)]
    sc = [GX[i, 24:32, :] for i in range(nx)]
    flow, weight = coarse_flow(base, kc, 1.0 / 8)
    rhs = [sc[i] * base[i] - flow[i] + cres[i] for i in range(nx)]
    z = [base[i] + cres[i] / (sc[i] + weight[i]) for i in range(nx)]
    for sweep in range(1, CSWEEPS):
        flow, weight = coarse_flow(z, kc, 1.0 / 8)
        z = [z[i] + (rhs[i] - sc[i] * z[i] + flow[i]) / (sc[i] + weight[i]) for i in range(nx)]
    for i in range(nx):
        CR[i, :, :] = z[i] - base[i]
    spread = jnp.where(
        iota((width, 128), 0) == 16 * me["gz"] + iota((width, 128), 1) // 8, 1.0, 0.0
    ).astype(F32)
    wide = jnp.dot(
        CR[me["gx"]], spread, precision=lax.Precision.HIGHEST, preferred_element_type=F32
    )
    sub = iota((8, 128), 0)
    for j in range(2):
        line = jnp.sum(jnp.where(sub == 2 * me["gy"] + j, wide, 0.0), axis=0, keepdims=True)
        for y in range(8 * j, 8 * j + 8):
            out[pl.ds(y, 8, stride=16), :] = CB[8 * y : 8 * y + 8, :] + line
    for copy in sent:
        copy.wait_send()


def shards(sizes, *args):
    nx, ny, nz = sizes
    width = max(128, 16 * nz)
    field = lambda *lead: pltpu.VMEM(lead + (3, ROWS, 128), F32)
    links = nx + ny + nz - 3
    scratch = [
        pltpu.VMEM((4, 128, 128), F32),
        pltpu.VMEM((4, 2, 64, 128), F32),
        pltpu.VMEM((4, 384, 128), F32),
        field(4),
        pltpu.VMEM((2, 2, 3, 8, 128), F32),
        pltpu.VMEM((2, 2, 3, 8, 128), F32),
        field(), field(), field(), field(), field(), field(), field(2),
        pltpu.VMEM((384, 128), F32),
        pltpu.VMEM((128, 128), F32),
        pltpu.VMEM((2, 16, 128), F32),
        pltpu.VMEM((2, 16, 128), F32),
        pltpu.VMEM((2, 8, 128), F32),
        pltpu.VMEM((16, 128), F32),
        pltpu.VMEM((2, 16, 128), F32),
        pltpu.VMEM((8, 128), F32),
        pltpu.VMEM((nz, 8, 128), F32),
        pltpu.VMEM((8, width), F32),
        pltpu.VMEM((ny, 8, width), F32),
        pltpu.VMEM((32, width), F32),
        pltpu.VMEM((nx, 32, width), F32),
        pltpu.VMEM((nx, 8, width), F32),
    ] + [pltpu.SemaphoreType.DMA((n,)) for n in (4, 8, 8, 8, 8, 4, 4, 6, 6, links, links)]
    out = pl.pallas_call(
        functools.partial(kernel, sizes),
        out_shape=jax.ShapeDtypeStruct((128, 128), F32),
        in_specs=[pl.BlockSpec(memory_space=pl.ANY)] * 4,
        out_specs=pl.BlockSpec(memory_space=pltpu.VMEM),
        scratch_shapes=scratch,
        compiler_params=pltpu.CompilerParams(
            collective_id=0, has_side_effects=True, vmem_limit_bytes=24 * 1024 * 1024
        ),
    )(*[x.reshape(128, 128) for x in args])
    return out.reshape(8, 16, 128)


def solution(mesh):
    spec = P(*AXES)
    sizes = tuple(mesh.shape[name] for name in AXES)
    return jax.shard_map(
        functools.partial(shards, sizes), mesh=mesh, in_specs=(spec,) * 4, out_specs=spec, check_vma=False
    )
```

```python
import functools

import jax
import jax.numpy as jnp
from jax import lax
from jax.experimental import pallas as pl
from jax.experimental.pallas import tpu as pltpu
from jax.sharding import PartitionSpec as P

NEWTON = 2
SWEEPS = 4
CSWEEPS = 6
AXES = ("gx", "gy", "gz")
F32 = jnp.float32
ROWS = 152
FIRST = 8
LAST = 144
CHUNK = 16
ITER, SRC, PERM, STORE = 0, 1, 2, 3
ORDER = (ITER, PERM, SRC, STORE)


def g(d):
    y = d * d + 1.0
    r = lax.rsqrt(y)
    return lax.rsqrt(y * r)


def iota(shape, dim):
    return lax.broadcasted_iota(jnp.int32, shape, dim)


def roll(v, shift, axis):
    return pltpu.roll(v, shift % v.shape[axis], axis)


def y_up(tiles):
    rolled = [roll(v, -16, 1) for v in tiles]
    inside = iota(tiles[0].shape, 1) < 112
    return [jnp.where(inside, rolled[t], rolled[(t + 1) % 3]) for t in range(3)]


def y_down(tiles):
    rolled = [roll(v, 16, 1) for v in tiles]
    inside = iota(tiles[0].shape, 1) >= 16
    return [jnp.where(inside, rolled[t], rolled[(t - 1) % 3]) for t in range(3)]


def chunks():
    at = FIRST
    while at < LAST:
        size = min(CHUNK, LAST - at)
        yield at, size
        at += size


def newton(T, AX, AY, AZ, FZ, RES, RD, D):
    for it in range(NEWTON):
        for r, n in chunks():
            v = [T[ITER, t, r : r + n, :] for t in range(3)]
            k = [T[PERM, t, r : r + n, :] for t in range(3)]
            vy, ky = y_up(v), y_up(k)
            ay, fy, ax, fx = [], [], [], []
            for t in range(3):
                d = vy[t] - v[t]
                a = (0.5 * (ky[t] + k[t])) * g(d)
                AY[t, r : r + n, :] = a
                ay.append(a)
                fy.append(a * d)
                d = roll(v[t], -1, 1) - v[t]
                a = (0.5 * (roll(k[t], -1, 1) + k[t])) * g(d)
                AX[t, r : r + n, :] = a
                ax.append(a)
                fx.append(a * d)
            aym, fym = y_down(ay), y_down(fy)
            lane = iota((n, 128), 1)
            row = iota((n, 128), 0) + (r - FIRST)
            x, yl = lane % 16, lane // 16
            for t in range(3):
                d = T[ITER, t, r + 1 : r + n + 1, :] - v[t]
                az = (0.5 * (T[PERM, t, r + 1 : r + n + 1, :] + k[t])) * g(d)
                fz = az * d
                AZ[t, r : r + n, :] = az
                FZ[t, r : r + n, :] = fz
                azm = AZ[t, r - 1 : r + n - 1, :]
                fzm = FZ[t, r - 1 : r + n - 1, :]
                flow = (fz - fzm) + (fy[t] - fym[t]) + (fx[t] - roll(fx[t], 1, 1))
                weight = (az + azm) + (ay[t] + aym[t]) + (ax[t] + roll(ax[t], 1, 1))
                c = T[STORE, t, r : r + n, :]
                res = T[SRC, t, r : r + n, :] - c * v[t] + flow
                y = yl + 8 * t
                known = (x >= 1) & (x <= 14) & (y >= 1) & (y <= 22) & (row >= 1) & (row <= 134)
                rd = jnp.where(known, 1.0 / (c + weight), 0.0)
                RES[t, r : r + n, :] = res
                RD[t, r : r + n, :] = rd
                D[0, t, r : r + n, :] = res * rd
        for sweep in range(SWEEPS - 1):
            old, new = sweep % 2, (sweep + 1) % 2
            for r, n in chunks():
                d = [D[old, t, r : r + n, :] for t in range(3)]
                ay = [AY[t, r : r + n, :] for t in range(3)]
                up = y_up(d)
                down = y_down([ay[t] * d[t] for t in range(3)])
                for t in range(3):
                    ax = AX[t, r : r + n, :]
                    total = RES[t, r : r + n, :] + ay[t] * up[t] + down[t]
                    total += ax * roll(d[t], -1, 1) + roll(ax * d[t], 1, 1)
                    total += AZ[t, r : r + n, :] * D[old, t, r + 1 : r + n + 1, :]
                    total += AZ[t, r - 1 : r + n - 1, :] * D[old, t, r - 1 : r + n - 1, :]
                    delta = total * RD[t, r : r + n, :]
                    if sweep < SWEEPS - 2:
                        D[new, t, r : r + n, :] = delta
                    else:
                        T[ITER, t, r : r + n, :] = T[ITER, t, r : r + n, :] + delta


def coarse_flow(z, k, inv):
    n = len(z)
    flow, weight = [], []
    up = []
    for i in range(n):
        d = z[(i + 1) % n] - z[i]
        a = (0.5 * inv * inv * (k[(i + 1) % n] + k[i])) * g(d * inv)
        up.append((a, a * d))
    for i in range(n):
        a, f = up[i]
        am, fm = up[i - 1]
        w, fl = a + am, f - fm
        for axis in range(2):
            d = roll(z[i], -1, axis) - z[i]
            a = (0.5 * inv * inv * (roll(k[i], -1, axis) + k[i])) * g(d * inv)
            f = a * d
            w = w + (a + roll(a, 1, axis))
            fl = fl + (f - roll(f, 1, axis))
        flow.append(fl)
        weight.append(w)
    return flow, weight


def reaches(sizes):
    rx, ry, rz = (n // 2 for n in sizes)
    spare = max(rx - 1, 0) + max(ry - 1, 0) + max(rz - 1, 0)
    return spare <= 2 and 16 * sizes[2] <= 128


def kernel(
    sizes, it_ref, src_ref, perm_ref, store_ref, out,
    I, XR, PA, T, ZS, ZR, AX, AY, AZ, FZ, RES, RD, D, Q, CB, XS, XF, YF, FS, ZF,
    GS, GA, GZ, GM, GY, GV, GX, CR,
    lsem, xs_sem, xr_sem, ys_sem, yr_sem, zs_sem, zr_sem, fs_sem, fr_sem, gs_sem, gr_sem,
):
    nx, ny, nz = sizes
    size = dict(zip(AXES, sizes))
    direct = reaches(sizes)
    me = {name: lax.axis_index(name) for name in AXES}

    def there(name, step):
        return {name: lax.rem(me[name] + (step + size[name]), size[name])}

    def send(src, dst, s, r, name, step):
        copy = pltpu.make_async_remote_copy(
            src_ref=src, dst_ref=dst, send_sem=s, recv_sem=r,
            device_id=there(name, step), device_id_type=pl.DeviceIdType.MESH,
        )
        copy.start()
        return copy

    barrier = pltpu.get_barrier_semaphore()
    greeted = [(name, step) for name in AXES for step in (1, -1)]
    if not direct:
        greeted = [(name, step) for name in AXES for step in range(1, size[name])]
    for name, step in greeted:
        pl.semaphore_signal(
            barrier, inc=1, device_id=there(name, step), device_id_type=pl.DeviceIdType.MESH
        )
    local = {}
    for a, ref in enumerate((it_ref, src_ref, perm_ref, store_ref)):
        local[a] = pltpu.make_async_copy(ref, I.at[a], lsem.at[a])
        local[a].start()
    for buf in (T,):
        for a in range(4):
            for t in range(3):
                buf[a, t, 0:FIRST, :] = jnp.zeros((FIRST, 128), F32)
                buf[a, t, LAST:ROWS, :] = jnp.zeros((ROWS - LAST, 128), F32)
    for buf in (AZ, FZ):
        for t in range(3):
            buf[t, 0:FIRST, :] = jnp.zeros((FIRST, 128), F32)
    for b in range(2):
        for t in range(3):
            D[b, t, 0:FIRST, :] = jnp.zeros((FIRST, 128), F32)
            D[b, t, LAST:ROWS, :] = jnp.zeros((ROWS - LAST, 128), F32)
    for a in range(4):
        local[a].wait()
    pl.semaphore_wait(barrier, len(greeted))

    sent = []
    xcopy, ycopy, zcopy = {}, {}, {}
    for a in ORDER:
        hi = send(I.at[a, pl.ds(64, 64)], XR.at[a, 0], xs_sem.at[2 * a], xr_sem.at[2 * a], "gx", 1)
        lo = send(I.at[a, pl.ds(0, 64)], XR.at[a, 1], xs_sem.at[2 * a + 1], xr_sem.at[2 * a + 1], "gx", -1)
        xcopy[a] = (hi, lo)
        sent += [hi, lo]
    for a in ORDER:
        for x in range(8):
            PA[a, pl.ds(64 + 4 + x, 16, stride=16), :] = I[a, 16 * x : 16 * x + 16, :]
    for a in ORDER:
        for side in range(2):
            xcopy[a][side].wait_recv()
            for x in range(4):
                PA[a, pl.ds(64 + 12 * side + x, 16, stride=16), :] = XR[a, side, 16 * x : 16 * x + 16, :]
        hi = send(PA.at[a, pl.ds(256, 64)], PA.at[a, pl.ds(0, 64)], ys_sem.at[2 * a], yr_sem.at[2 * a], "gy", 1)
        lo = send(PA.at[a, pl.ds(64, 64)], PA.at[a, pl.ds(320, 64)], ys_sem.at[2 * a + 1], yr_sem.at[2 * a + 1], "gy", -1)
        ycopy[a] = (hi, lo)
        sent += [hi, lo]
    for p in range(2):
        for h in range(2):
            a = ORDER[2 * p + h]
            ycopy[a][0].wait_recv()
            ycopy[a][1].wait_recv()
            for t in range(3):
                m = PA[a, 128 * t : 128 * t + 128, :].T
                T[a, t, 12:140, :] = m
                ZS[p, 0, t, 4 * h : 4 * h + 4, :] = m[124:128, :]
                ZS[p, 1, t, 4 * h : 4 * h + 4, :] = m[0:4, :]
        hi = send(ZS.at[p, 0], ZR.at[p, 0], zs_sem.at[2 * p], zr_sem.at[2 * p], "gz", 1)
        lo = send(ZS.at[p, 1], ZR.at[p, 1], zs_sem.at[2 * p + 1], zr_sem.at[2 * p + 1], "gz", -1)
        zcopy[p] = (hi, lo)
        sent += [hi, lo]
    for p in range(2):
        zcopy[p][0].wait_recv()
        zcopy[p][1].wait_recv()
        for h in range(2):
            a = ORDER[2 * p + h]
            for t in range(3):
                T[a, t, 8:12, :] = ZR[p, 0, t, 4 * h : 4 * h + 4, :]
                T[a, t, 140:144, :] = ZR[p, 1, t, 4 * h : 4 * h + 4, :]

    newton(T, AX, AY, AZ, FZ, RES, RD, D)

    for t in range(3):
        Q[128 * t : 128 * t + 128, :] = T[ITER, t, 12:140, :].T
    lane = iota((8, 128), 1)
    pack_c = jnp.zeros((8, 128), F32)
    pack_k = jnp.zeros((8, 128), F32)
    for y in range(16):
        b = (y + 4) * 16 + 4
        c = Q[b : b + 8, :]
        CB[8 * y : 8 * y + 8, :] = c
        pack_c = jnp.where(lane // 2 == y, roll(c, 1 + 2 * y, 1), pack_c)
        pack_k = jnp.where(lane // 2 == y, roll(PA[PERM, b : b + 8, :], 1 + 2 * y, 1), pack_k)
    XS[0, :, :] = Q[pl.ds(64 + 11, 16, stride=16), :]
    XS[1, :, :] = Q[pl.ds(64 + 4, 16, stride=16), :]
    FS[0:8, :] = pack_c
    FS[8:16, :] = pack_k
    faces = [
        send(XS.at[0], XF.at[0], fs_sem.at[0], fr_sem.at[0], "gx", 1),
        send(XS.at[1], XF.at[1], fs_sem.at[1], fr_sem.at[1], "gx", -1),
        send(CB.at[pl.ds(120, 8)], YF.at[0], fs_sem.at[2], fr_sem.at[2], "gy", 1),
        send(CB.at[pl.ds(0, 8)], YF.at[1], fs_sem.at[3], fr_sem.at[3], "gy", -1),
        send(FS, ZF.at[0], fs_sem.at[4], fr_sem.at[4], "gz", 1),
        send(FS, ZF.at[1], fs_sem.at[5], fr_sem.at[5], "gz", -1),
    ]
    sent += faces
    for copy in faces:
        copy.wait_recv()
    Q[pl.ds(64 + 3, 16, stride=16), :] = XF[0, :, :]
    Q[pl.ds(64 + 12, 16, stride=16), :] = XF[1, :, :]
    Q[3 * 16 + 4 : 3 * 16 + 12, :] = YF[0, :, :]
    Q[20 * 16 + 4 : 20 * 16 + 12, :] = YF[1, :, :]

    sums = [[None, None] for _ in range(4)]

    def add(q, j, value):
        sums[q][j] = value if sums[q][j] is None else sums[q][j] + value

    zf = [ZF[0, 0:8, :], ZF[1, 0:8, :]]
    zk = [ZF[0, 8:16, :], ZF[1, 8:16, :]]
    for y in range(16):
        b = (y + 4) * 16 + 4
        c, k = Q[b : b + 8, :], PA[PERM, b : b + 8, :]
        near = [(Q[b + o : b + o + 8, :], PA[PERM, b + o : b + o + 8, :]) for o in (1, -1, 16, -16)]
        near.append(tuple(
            jnp.where(lane == 127, roll(far, 126 - 2 * y, 1), roll(own, -1, 1))
            for far, own in ((zf[1], c), (zk[1], k))
        ))
        near.append(tuple(
            jnp.where(lane == 0, roll(far, -2 * y, 1), roll(own, 1, 1))
            for far, own in ((zf[0], c), (zk[0], k))
        ))
        flow = 0.0
        for cn, kn in near:
            d = cn - c
            flow = flow + (0.5 * (k + kn)) * g(d) * d
        st = PA[STORE, b : b + 8, :]
        j = y // 8
        add(0, j, c)
        add(1, j, PA[SRC, b : b + 8, :] - st * c + flow)
        add(2, j, k)
        add(3, j, st)
    rows = [jnp.sum(sums[q][j], axis=0, keepdims=True) for q in range(4) for j in range(2)]
    mean = jnp.where(iota((128, 128), 0) // 8 == iota((128, 128), 1) % 16, 1.0 / 512, 0.0).astype(F32)
    tile = jnp.dot(
        jnp.concatenate(rows, axis=0), mean,
        precision=lax.Precision.HIGHEST, preferred_element_type=F32,
    )

    width = GM.shape[-1]

    def gather(src, buf, name, base):
        n = size[name]
        copies = [
            send(src, buf.at[me[name]], gs_sem.at[base + s - 1], gr_sem.at[base + s - 1], name, s)
            for s in range(1, n)
        ]
        buf[me[name]] = src[...]
        for copy in copies:
            copy.wait_recv()
        sent.extend(copies)

    if direct:
        def at(i, j, k):
            return (i * ny + j) * nz + k

        GS[...] = tile
        mine = at(*[me[name] for name in AXES])
        copies = []
        for i in range(nx):
            for j in range(ny):
                for k in range(nz):
                    if i + j + k:
                        copy = pltpu.make_async_remote_copy(
                            src_ref=GS, dst_ref=GA.at[mine],
                            send_sem=gs_sem.at[len(copies)], recv_sem=gr_sem.at[len(copies)],
                            device_id=tuple(
                                lax.rem(me[name] + step, size[name])
                                for name, step in zip(AXES, (i, j, k))
                            ),
                            device_id_type=pl.DeviceIdType.MESH,
                        )
                        copy.start()
                        copies.append(copy)
        GA[mine] = tile
        for copy in copies:
            copy.wait_recv()
        sent.extend(copies)
        wlane = iota((8, 128), 1)
        for i in range(nx):
            for j in range(ny):
                merged = GA[at(i, j, 0)]
                for k in range(1, nz):
                    merged = jnp.where((wlane // 16) % nz == k, GA[at(i, j, k)], merged)
                for q in range(4):
                    GX[i, 8 * q + 2 * j : 8 * q + 2 * j + 2, :] = merged[2 * q : 2 * q + 2, :]
    else:
        GS[...] = tile
        gather(GS, GZ, "gz", 0)
        wlane = iota((8, width), 1)
        merged = None
        for z in range(nz):
            part = GZ[z]
            if width > 128:
                part = jnp.concatenate([part] * (width // 128), axis=1)
            merged = part if merged is None else jnp.where((wlane // 16) % nz == z, part, merged)
        GM[...] = merged
        gather(GM, GY, "gy", nz - 1)
        for y in range(ny):
            for q in range(4):
                GV[8 * q + 2 * y : 8 * q + 2 * y + 2, :] = GY[y, 2 * q : 2 * q + 2, :]
        gather(GV, GX, "gx", nz + ny - 2)

    base = [GX[i, 0:8, :] for i in range(nx)]
    cres = [GX[i, 8:16, :] for i in range(nx)]
    kc = [GX[i, 16:24, :] for i in range(nx)]
    sc = [GX[i, 24:32, :] for i in range(nx)]
    flow, weight = coarse_flow(base, kc, 1.0 / 8)
    rhs = [sc[i] * base[i] - flow[i] + cres[i] for i in range(nx)]
    z = [base[i] + cres[i] / (sc[i] + weight[i]) for i in range(nx)]
    for sweep in range(1, CSWEEPS):
        flow, weight = coarse_flow(z, kc, 1.0 / 8)
        z = [z[i] + (rhs[i] - sc[i] * z[i] + flow[i]) / (sc[i] + weight[i]) for i in range(nx)]
    for i in range(nx):
        CR[i, :, :] = z[i] - base[i]
    spread = jnp.where(
        iota((width, 128), 0) == 16 * me["gz"] + iota((width, 128), 1) // 8, 1.0, 0.0
    ).astype(F32)
    wide = jnp.dot(
        CR[me["gx"]], spread, precision=lax.Precision.HIGHEST, preferred_element_type=F32
    )
    sub = iota((8, 128), 0)
    for j in range(2):
        line = jnp.sum(jnp.where(sub == 2 * me["gy"] + j, wide, 0.0), axis=0, keepdims=True)
        for y in range(8 * j, 8 * j + 8):
            out[pl.ds(y, 8, stride=16), :] = CB[8 * y : 8 * y + 8, :] + line
    for copy in sent:
        copy.wait_send()


def shards(sizes, *args):
    nx, ny, nz = sizes
    width = max(128, 16 * nz)
    field = lambda *lead: pltpu.VMEM(lead + (3, ROWS, 128), F32)
    direct = reaches(sizes)
    links = nx * ny * nz - 1 if direct else nx + ny + nz - 3
    scratch = [
        pltpu.VMEM((4, 128, 128), F32),
        pltpu.VMEM((4, 2, 64, 128), F32),
        pltpu.VMEM((4, 384, 128), F32),
        field(4),
        pltpu.VMEM((2, 2, 3, 8, 128), F32),
        pltpu.VMEM((2, 2, 3, 8, 128), F32),
        field(), field(), field(), field(), field(), field(), field(2),
        pltpu.VMEM((384, 128), F32),
        pltpu.VMEM((128, 128), F32),
        pltpu.VMEM((2, 16, 128), F32),
        pltpu.VMEM((2, 16, 128), F32),
        pltpu.VMEM((2, 8, 128), F32),
        pltpu.VMEM((16, 128), F32),
        pltpu.VMEM((2, 16, 128), F32),
        pltpu.VMEM((8, 128), F32),
        pltpu.VMEM((nx * ny * nz if direct else 1, 8, 128), F32),
        pltpu.VMEM((nz, 8, 128), F32),
        pltpu.VMEM((8, width), F32),
        pltpu.VMEM((ny, 8, width), F32),
        pltpu.VMEM((32, width), F32),
        pltpu.VMEM((nx, 32, width), F32),
        pltpu.VMEM((nx, 8, width), F32),
    ] + [pltpu.SemaphoreType.DMA((n,)) for n in (4, 8, 8, 8, 8, 4, 4, 6, 6, links, links)]
    out = pl.pallas_call(
        functools.partial(kernel, sizes),
        out_shape=jax.ShapeDtypeStruct((128, 128), F32),
        in_specs=[pl.BlockSpec(memory_space=pl.ANY)] * 4,
        out_specs=pl.BlockSpec(memory_space=pltpu.VMEM),
        scratch_shapes=scratch,
        compiler_params=pltpu.CompilerParams(
            collective_id=0, has_side_effects=True, vmem_limit_bytes=60 * 1024 * 1024
        ),
    )(*[x.reshape(128, 128) for x in args])
    return out.reshape(8, 16, 128)


def solution(mesh):
    spec = P(*AXES)
    sizes = tuple(mesh.shape[name] for name in AXES)
    return jax.shard_map(
        functools.partial(shards, sizes), mesh=mesh, in_specs=(spec,) * 4, out_specs=spec, check_vma=False
    )
```

```python
import functools

import jax
import jax.numpy as jnp
from jax import lax
from jax.experimental import pallas as pl
from jax.experimental.pallas import tpu as pltpu
from jax.sharding import PartitionSpec as P

NEWTON = 2
SWEEPS = 4
CSWEEPS = 6
AXES = ("gx", "gy", "gz")
F32 = jnp.float32
ROWS = 152
FIRST = 8
LAST = 144
CHUNK = 16
ITER, SRC, PERM, STORE = 0, 1, 2, 3
ORDER = (ITER, PERM, SRC, STORE)


def g(d):
    y = d * d + 1.0
    r = lax.rsqrt(y)
    return lax.rsqrt(y * r)


def iota(shape, dim):
    return lax.broadcasted_iota(jnp.int32, shape, dim)


def roll(v, shift, axis):
    return pltpu.roll(v, shift % v.shape[axis], axis)


def y_up(tiles):
    rolled = [roll(v, -16, 1) for v in tiles]
    inside = iota(tiles[0].shape, 1) < 112
    return [jnp.where(inside, rolled[t], rolled[(t + 1) % 3]) for t in range(3)]


def y_down(tiles):
    rolled = [roll(v, 16, 1) for v in tiles]
    inside = iota(tiles[0].shape, 1) >= 16
    return [jnp.where(inside, rolled[t], rolled[(t - 1) % 3]) for t in range(3)]


def chunks():
    at = FIRST
    while at < LAST:
        size = min(CHUNK, LAST - at)
        yield at, size
        at += size


def newton(T, AX, AY, AZ, FZ, RES, RD, D):
    for it in range(NEWTON):
        for r, n in chunks():
            v = [T[ITER, t, r : r + n, :] for t in range(3)]
            k = [T[PERM, t, r : r + n, :] for t in range(3)]
            vy, ky = y_up(v), y_up(k)
            ay, fy, ax, fx = [], [], [], []
            for t in range(3):
                d = vy[t] - v[t]
                a = (0.5 * (ky[t] + k[t])) * g(d)
                AY[t, r : r + n, :] = a
                ay.append(a)
                fy.append(a * d)
                d = roll(v[t], -1, 1) - v[t]
                a = (0.5 * (roll(k[t], -1, 1) + k[t])) * g(d)
                AX[t, r : r + n, :] = a
                ax.append(a)
                fx.append(a * d)
            aym, fym = y_down(ay), y_down(fy)
            lane = iota((n, 128), 1)
            row = iota((n, 128), 0) + (r - FIRST)
            x, yl = lane % 16, lane // 16
            for t in range(3):
                d = T[ITER, t, r + 1 : r + n + 1, :] - v[t]
                az = (0.5 * (T[PERM, t, r + 1 : r + n + 1, :] + k[t])) * g(d)
                fz = az * d
                AZ[t, r : r + n, :] = az
                FZ[t, r : r + n, :] = fz
                azm = AZ[t, r - 1 : r + n - 1, :]
                fzm = FZ[t, r - 1 : r + n - 1, :]
                flow = (fz - fzm) + (fy[t] - fym[t]) + (fx[t] - roll(fx[t], 1, 1))
                weight = (az + azm) + (ay[t] + aym[t]) + (ax[t] + roll(ax[t], 1, 1))
                c = T[STORE, t, r : r + n, :]
                res = T[SRC, t, r : r + n, :] - c * v[t] + flow
                y = yl + 8 * t
                known = (x >= 1) & (x <= 14) & (y >= 1) & (y <= 22) & (row >= 1) & (row <= 134)
                rd = jnp.where(known, 1.0 / (c + weight), 0.0)
                RES[t, r : r + n, :] = res
                RD[t, r : r + n, :] = rd
                D[0, t, r : r + n, :] = res * rd
        for sweep in range(SWEEPS - 1):
            old, new = sweep % 2, (sweep + 1) % 2
            for r, n in chunks():
                d = [D[old, t, r : r + n, :] for t in range(3)]
                ay = [AY[t, r : r + n, :] for t in range(3)]
                up = y_up(d)
                down = y_down([ay[t] * d[t] for t in range(3)])
                for t in range(3):
                    ax = AX[t, r : r + n, :]
                    total = RES[t, r : r + n, :] + ay[t] * up[t] + down[t]
                    total += ax * roll(d[t], -1, 1) + roll(ax * d[t], 1, 1)
                    total += AZ[t, r : r + n, :] * D[old, t, r + 1 : r + n + 1, :]
                    total += AZ[t, r - 1 : r + n - 1, :] * D[old, t, r - 1 : r + n - 1, :]
                    delta = total * RD[t, r : r + n, :]
                    if sweep < SWEEPS - 2:
                        D[new, t, r : r + n, :] = delta
                    else:
                        T[ITER, t, r : r + n, :] = T[ITER, t, r : r + n, :] + delta


def coarse_flow(z, k, inv):
    n = len(z)
    flow, weight = [], []
    up = []
    for i in range(n):
        d = z[(i + 1) % n] - z[i]
        a = (0.5 * inv * inv * (k[(i + 1) % n] + k[i])) * g(d * inv)
        up.append((a, a * d))
    for i in range(n):
        a, f = up[i]
        am, fm = up[i - 1]
        w, fl = a + am, f - fm
        for axis in range(2):
            d = roll(z[i], -1, axis) - z[i]
            a = (0.5 * inv * inv * (roll(k[i], -1, axis) + k[i])) * g(d * inv)
            f = a * d
            w = w + (a + roll(a, 1, axis))
            fl = fl + (f - roll(f, 1, axis))
        flow.append(fl)
        weight.append(w)
    return flow, weight


def reaches(sizes):
    rx, ry, rz = (n // 2 for n in sizes)
    spare = max(rx - 1, 0) + max(ry - 1, 0) + max(rz - 1, 0)
    return spare <= 2 and 16 * sizes[2] <= 128


def kernel(
    sizes, it_ref, src_ref, perm_ref, store_ref, out,
    I, XR, XP, PR, PA, T, ZS, ZR, AX, AY, AZ, FZ, RES, RD, D, Q, CB, XS, XF, YF, FS, ZF,
    GS, GA, GZ, GM, GY, GV, GX, CR,
    lsem, xs_sem, xr_sem, ys_sem, yr_sem, ps_sem, pr_sem, zs_sem, zr_sem, fs_sem, fr_sem, gs_sem, gr_sem,
):
    nx, ny, nz = sizes
    size = dict(zip(AXES, sizes))
    direct = reaches(sizes)
    me = {name: lax.axis_index(name) for name in AXES}

    def there(name, step):
        return {name: lax.rem(me[name] + (step + size[name]), size[name])}

    def send(src, dst, s, r, name, step):
        copy = pltpu.make_async_remote_copy(
            src_ref=src, dst_ref=dst, send_sem=s, recv_sem=r,
            device_id=there(name, step), device_id_type=pl.DeviceIdType.MESH,
        )
        copy.start()
        return copy

    barrier = pltpu.get_barrier_semaphore()
    greeted = [(name, step) for name in AXES for step in (1, -1)]
    if not direct:
        greeted = [(name, step) for name in AXES for step in range(1, size[name])]
    for name, step in greeted:
        pl.semaphore_signal(
            barrier, inc=1, device_id=there(name, step), device_id_type=pl.DeviceIdType.MESH
        )
    local = {}
    for a, ref in enumerate((it_ref, src_ref, perm_ref, store_ref)):
        local[a] = pltpu.make_async_copy(ref, I.at[a], lsem.at[a])
        local[a].start()
    for buf in (T,):
        for a in range(4):
            for t in range(3):
                buf[a, t, 0:FIRST, :] = jnp.zeros((FIRST, 128), F32)
                buf[a, t, LAST:ROWS, :] = jnp.zeros((ROWS - LAST, 128), F32)
    for buf in (AZ, FZ):
        for t in range(3):
            buf[t, 0:FIRST, :] = jnp.zeros((FIRST, 128), F32)
    for b in range(2):
        for t in range(3):
            D[b, t, 0:FIRST, :] = jnp.zeros((FIRST, 128), F32)
            D[b, t, LAST:ROWS, :] = jnp.zeros((ROWS - LAST, 128), F32)
    for a in range(4):
        local[a].wait()
    pl.semaphore_wait(barrier, len(greeted))

    sent = []
    xcopy, ycopy, zcopy = {}, {}, {}

    def fill_own(a):
        for x in range(8):
            PA[a, pl.ds(64 + 4 + x, 16, stride=16), :] = I[a, 16 * x : 16 * x + 16, :]

    def send_x(a, planes):
        n = 16 * planes
        hi = send(I.at[a, pl.ds(128 - n, n)], XR.at[a, 0, pl.ds(64 - n, n)], xs_sem.at[2 * a], xr_sem.at[2 * a], "gx", 1)
        lo = send(I.at[a, pl.ds(0, n)], XR.at[a, 1, pl.ds(0, n)], xs_sem.at[2 * a + 1], xr_sem.at[2 * a + 1], "gx", -1)
        xcopy[a] = (hi, lo)
        sent.extend([hi, lo])

    def fill_x(a, planes):
        for side in range(2):
            xcopy[a][side].wait_recv()
            for x in range(4 - planes, 4) if side == 0 else range(planes):
                PA[a, pl.ds(64 + 12 * side + x, 16, stride=16), :] = XR[a, side, 16 * x : 16 * x + 16, :]

    def send_y(a):
        hi = send(PA.at[a, pl.ds(256, 64)], PA.at[a, pl.ds(0, 64)], ys_sem.at[2 * a], yr_sem.at[2 * a], "gy", 1)
        lo = send(PA.at[a, pl.ds(64, 64)], PA.at[a, pl.ds(320, 64)], ys_sem.at[2 * a + 1], yr_sem.at[2 * a + 1], "gy", -1)
        ycopy[a] = (hi, lo)

    first, second = ORDER[:2], ORDER[2:]
    for a in first:
        send_x(a, 4)
    for a in second:
        fill_own(a)
        for x in (0, 15):
            PA[a, pl.ds(64 + x, 16, stride=16), :] = jnp.zeros((16, 128), F32)
        send_y(a)
    for a in second:
        send_x(a, 3)
    for a in first:
        fill_own(a)
    pieces = {}
    for n, a in enumerate(second):
        for copy in ycopy[a]:
            copy.wait_recv()
        for p in range(3):
            for side in range(2):
                x = (9, 4)[side] + p
                XP[n, side, 8 * p : 8 * p + 4, :] = PA[a, pl.ds(x, 4, stride=16), :]
                XP[n, side, 8 * p + 4 : 8 * p + 8, :] = PA[a, pl.ds(320 + x, 4, stride=16), :]
        pieces[a] = [
            send(XP.at[n, side], PR.at[n, side], ps_sem.at[2 * n + side], pr_sem.at[2 * n + side], "gx", (1, -1)[side])
            for side in range(2)
        ]
        sent.extend(pieces[a])
    for a in first:
        fill_x(a, 4)
        send_y(a)
        sent.extend(ycopy[a])

    def arrive(n, a):
        if a in first:
            for copy in ycopy[a]:
                copy.wait_recv()
            return
        for copy in ycopy[a]:
            copy.wait_send()
        fill_x(a, 3)
        for side in range(2):
            pieces[a][side].wait_recv()
            for p in range(3):
                x = (1, 12)[side] + p
                PA[a, pl.ds(x, 4, stride=16), :] = PR[n, side, 8 * p : 8 * p + 4, :]
                PA[a, pl.ds(320 + x, 4, stride=16), :] = PR[n, side, 8 * p + 4 : 8 * p + 8, :]
        for x in (0, 15):
            PA[a, pl.ds(x, 4, stride=16), :] = jnp.zeros((4, 128), F32)
            PA[a, pl.ds(320 + x, 4, stride=16), :] = jnp.zeros((4, 128), F32)

    for p in range(2):
        for h in range(2):
            a = ORDER[2 * p + h]
            arrive(h, a)
            for t in range(3):
                m = PA[a, 128 * t : 128 * t + 128, :].T
                T[a, t, 12:140, :] = m
                ZS[p, 0, t, 4 * h : 4 * h + 4, :] = m[124:128, :]
                ZS[p, 1, t, 4 * h : 4 * h + 4, :] = m[0:4, :]
        hi = send(ZS.at[p, 0], ZR.at[p, 0], zs_sem.at[2 * p], zr_sem.at[2 * p], "gz", 1)
        lo = send(ZS.at[p, 1], ZR.at[p, 1], zs_sem.at[2 * p + 1], zr_sem.at[2 * p + 1], "gz", -1)
        zcopy[p] = (hi, lo)
        sent += [hi, lo]
    for p in range(2):
        zcopy[p][0].wait_recv()
        zcopy[p][1].wait_recv()
        for h in range(2):
            a = ORDER[2 * p + h]
            for t in range(3):
                T[a, t, 8:12, :] = ZR[p, 0, t, 4 * h : 4 * h + 4, :]
                T[a, t, 140:144, :] = ZR[p, 1, t, 4 * h : 4 * h + 4, :]

    newton(T, AX, AY, AZ, FZ, RES, RD, D)

    for t in range(3):
        Q[128 * t : 128 * t + 128, :] = T[ITER, t, 12:140, :].T
    lane = iota((8, 128), 1)
    pack_c = jnp.zeros((8, 128), F32)
    pack_k = jnp.zeros((8, 128), F32)
    for y in range(16):
        b = (y + 4) * 16 + 4
        c = Q[b : b + 8, :]
        CB[8 * y : 8 * y + 8, :] = c
        pack_c = jnp.where(lane // 2 == y, roll(c, 1 + 2 * y, 1), pack_c)
        pack_k = jnp.where(lane // 2 == y, roll(PA[PERM, b : b + 8, :], 1 + 2 * y, 1), pack_k)
    XS[0, :, :] = Q[pl.ds(64 + 11, 16, stride=16), :]
    XS[1, :, :] = Q[pl.ds(64 + 4, 16, stride=16), :]
    FS[0:8, :] = pack_c
    FS[8:16, :] = pack_k
    faces = [
        send(XS.at[0], XF.at[0], fs_sem.at[0], fr_sem.at[0], "gx", 1),
        send(XS.at[1], XF.at[1], fs_sem.at[1], fr_sem.at[1], "gx", -1),
        send(CB.at[pl.ds(120, 8)], YF.at[0], fs_sem.at[2], fr_sem.at[2], "gy", 1),
        send(CB.at[pl.ds(0, 8)], YF.at[1], fs_sem.at[3], fr_sem.at[3], "gy", -1),
        send(FS, ZF.at[0], fs_sem.at[4], fr_sem.at[4], "gz", 1),
        send(FS, ZF.at[1], fs_sem.at[5], fr_sem.at[5], "gz", -1),
    ]
    sent += faces
    for copy in faces:
        copy.wait_recv()
    Q[pl.ds(64 + 3, 16, stride=16), :] = XF[0, :, :]
    Q[pl.ds(64 + 12, 16, stride=16), :] = XF[1, :, :]
    Q[3 * 16 + 4 : 3 * 16 + 12, :] = YF[0, :, :]
    Q[20 * 16 + 4 : 20 * 16 + 12, :] = YF[1, :, :]

    sums = [[None, None] for _ in range(4)]

    def add(q, j, value):
        sums[q][j] = value if sums[q][j] is None else sums[q][j] + value

    zf = [ZF[0, 0:8, :], ZF[1, 0:8, :]]
    zk = [ZF[0, 8:16, :], ZF[1, 8:16, :]]
    for y in range(16):
        b = (y + 4) * 16 + 4
        c, k = Q[b : b + 8, :], PA[PERM, b : b + 8, :]
        near = [(Q[b + o : b + o + 8, :], PA[PERM, b + o : b + o + 8, :]) for o in (1, -1, 16, -16)]
        near.append(tuple(
            jnp.where(lane == 127, roll(far, 126 - 2 * y, 1), roll(own, -1, 1))
            for far, own in ((zf[1], c), (zk[1], k))
        ))
        near.append(tuple(
            jnp.where(lane == 0, roll(far, -2 * y, 1), roll(own, 1, 1))
            for far, own in ((zf[0], c), (zk[0], k))
        ))
        flow = 0.0
        for cn, kn in near:
            d = cn - c
            flow = flow + (0.5 * (k + kn)) * g(d) * d
        st = PA[STORE, b : b + 8, :]
        j = y // 8
        add(0, j, c)
        add(1, j, PA[SRC, b : b + 8, :] - st * c + flow)
        add(2, j, k)
        add(3, j, st)
    rows = [jnp.sum(sums[q][j], axis=0, keepdims=True) for q in range(4) for j in range(2)]
    mean = jnp.where(iota((128, 128), 0) // 8 == iota((128, 128), 1) % 16, 1.0 / 512, 0.0).astype(F32)
    tile = jnp.dot(
        jnp.concatenate(rows, axis=0), mean,
        precision=lax.Precision.HIGHEST, preferred_element_type=F32,
    )

    width = GM.shape[-1]

    def gather(src, buf, name, base):
        n = size[name]
        copies = [
            send(src, buf.at[me[name]], gs_sem.at[base + s - 1], gr_sem.at[base + s - 1], name, s)
            for s in range(1, n)
        ]
        buf[me[name]] = src[...]
        for copy in copies:
            copy.wait_recv()
        sent.extend(copies)

    if direct:
        def at(i, j, k):
            return (i * ny + j) * nz + k

        GS[...] = tile
        mine = at(*[me[name] for name in AXES])
        copies = []
        for i in range(nx):
            for j in range(ny):
                for k in range(nz):
                    if i + j + k:
                        copy = pltpu.make_async_remote_copy(
                            src_ref=GS, dst_ref=GA.at[mine],
                            send_sem=gs_sem.at[len(copies)], recv_sem=gr_sem.at[len(copies)],
                            device_id=tuple(
                                lax.rem(me[name] + step, size[name])
                                for name, step in zip(AXES, (i, j, k))
                            ),
                            device_id_type=pl.DeviceIdType.MESH,
                        )
                        copy.start()
                        copies.append(copy)
        GA[mine] = tile
        for copy in copies:
            copy.wait_recv()
        sent.extend(copies)
        wlane = iota((8, 128), 1)
        for i in range(nx):
            for j in range(ny):
                merged = GA[at(i, j, 0)]
                for k in range(1, nz):
                    merged = jnp.where((wlane // 16) % nz == k, GA[at(i, j, k)], merged)
                for q in range(4):
                    GX[i, 8 * q + 2 * j : 8 * q + 2 * j + 2, :] = merged[2 * q : 2 * q + 2, :]
    else:
        GS[...] = tile
        gather(GS, GZ, "gz", 0)
        wlane = iota((8, width), 1)
        merged = None
        for z in range(nz):
            part = GZ[z]
            if width > 128:
                part = jnp.concatenate([part] * (width // 128), axis=1)
            merged = part if merged is None else jnp.where((wlane // 16) % nz == z, part, merged)
        GM[...] = merged
        gather(GM, GY, "gy", nz - 1)
        for y in range(ny):
            for q in range(4):
                GV[8 * q + 2 * y : 8 * q + 2 * y + 2, :] = GY[y, 2 * q : 2 * q + 2, :]
        gather(GV, GX, "gx", nz + ny - 2)

    base = [GX[i, 0:8, :] for i in range(nx)]
    cres = [GX[i, 8:16, :] for i in range(nx)]
    kc = [GX[i, 16:24, :] for i in range(nx)]
    sc = [GX[i, 24:32, :] for i in range(nx)]
    flow, weight = coarse_flow(base, kc, 1.0 / 8)
    rhs = [sc[i] * base[i] - flow[i] + cres[i] for i in range(nx)]
    z = [base[i] + cres[i] / (sc[i] + weight[i]) for i in range(nx)]
    for sweep in range(1, CSWEEPS):
        flow, weight = coarse_flow(z, kc, 1.0 / 8)
        z = [z[i] + (rhs[i] - sc[i] * z[i] + flow[i]) / (sc[i] + weight[i]) for i in range(nx)]
    for i in range(nx):
        CR[i, :, :] = z[i] - base[i]
    spread = jnp.where(
        iota((width, 128), 0) == 16 * me["gz"] + iota((width, 128), 1) // 8, 1.0, 0.0
    ).astype(F32)
    wide = jnp.dot(
        CR[me["gx"]], spread, precision=lax.Precision.HIGHEST, preferred_element_type=F32
    )
    sub = iota((8, 128), 0)
    for j in range(2):
        line = jnp.sum(jnp.where(sub == 2 * me["gy"] + j, wide, 0.0), axis=0, keepdims=True)
        for y in range(8 * j, 8 * j + 8):
            out[pl.ds(y, 8, stride=16), :] = CB[8 * y : 8 * y + 8, :] + line
    for copy in sent:
        copy.wait_send()


def shards(sizes, *args):
    nx, ny, nz = sizes
    width = max(128, 16 * nz)
    field = lambda *lead: pltpu.VMEM(lead + (3, ROWS, 128), F32)
    direct = reaches(sizes)
    links = nx * ny * nz - 1 if direct else nx + ny + nz - 3
    scratch = [
        pltpu.VMEM((4, 128, 128), F32),
        pltpu.VMEM((4, 2, 64, 128), F32),
        pltpu.VMEM((2, 2, 24, 128), F32),
        pltpu.VMEM((2, 2, 24, 128), F32),
        pltpu.VMEM((4, 384, 128), F32),
        field(4),
        pltpu.VMEM((2, 2, 3, 8, 128), F32),
        pltpu.VMEM((2, 2, 3, 8, 128), F32),
        field(), field(), field(), field(), field(), field(), field(2),
        pltpu.VMEM((384, 128), F32),
        pltpu.VMEM((128, 128), F32),
        pltpu.VMEM((2, 16, 128), F32),
        pltpu.VMEM((2, 16, 128), F32),
        pltpu.VMEM((2, 8, 128), F32),
        pltpu.VMEM((16, 128), F32),
        pltpu.VMEM((2, 16, 128), F32),
        pltpu.VMEM((8, 128), F32),
        pltpu.VMEM((nx * ny * nz if direct else 1, 8, 128), F32),
        pltpu.VMEM((nz, 8, 128), F32),
        pltpu.VMEM((8, width), F32),
        pltpu.VMEM((ny, 8, width), F32),
        pltpu.VMEM((32, width), F32),
        pltpu.VMEM((nx, 32, width), F32),
        pltpu.VMEM((nx, 8, width), F32),
    ] + [pltpu.SemaphoreType.DMA((n,)) for n in (4, 8, 8, 8, 8, 4, 4, 4, 4, 6, 6, links, links)]
    out = pl.pallas_call(
        functools.partial(kernel, sizes),
        out_shape=jax.ShapeDtypeStruct((128, 128), F32),
        in_specs=[pl.BlockSpec(memory_space=pl.ANY)] * 4,
        out_specs=pl.BlockSpec(memory_space=pltpu.VMEM),
        scratch_shapes=scratch,
        compiler_params=pltpu.CompilerParams(
            collective_id=0, has_side_effects=True, vmem_limit_bytes=60 * 1024 * 1024
        ),
    )(*[x.reshape(128, 128) for x in args])
    return out.reshape(8, 16, 128)


def solution(mesh):
    spec = P(*AXES)
    sizes = tuple(mesh.shape[name] for name in AXES)
    return jax.shard_map(
        functools.partial(shards, sizes), mesh=mesh, in_specs=(spec,) * 4, out_specs=spec, check_vma=False
    )
```

```python
import functools

import jax
import jax.numpy as jnp
from jax import lax
from jax.experimental import pallas as pl
from jax.experimental.pallas import tpu as pltpu
from jax.sharding import PartitionSpec as P

NEWTON = 2
SWEEPS = 4
CSWEEPS = 6
AXES = ("gx", "gy", "gz")
F32 = jnp.float32
ROWS = 152
FIRST = 8
LAST = 144
CHUNK = 48
ITER, SRC, PERM, STORE = 0, 1, 2, 3
ORDER = (ITER, PERM, SRC, STORE)


def g(d):
    y = d * d + 1.0
    r = lax.rsqrt(y)
    return lax.rsqrt(y * r)


def iota(shape, dim):
    return lax.broadcasted_iota(jnp.int32, shape, dim)


def roll(v, shift, axis):
    return pltpu.roll(v, shift % v.shape[axis], axis)


def y_up(tiles):
    rolled = [roll(v, -16, 1) for v in tiles]
    inside = iota(tiles[0].shape, 1) < 112
    return [jnp.where(inside, rolled[t], rolled[(t + 1) % 3]) for t in range(3)]


def y_down(tiles):
    rolled = [roll(v, 16, 1) for v in tiles]
    inside = iota(tiles[0].shape, 1) >= 16
    return [jnp.where(inside, rolled[t], rolled[(t - 1) % 3]) for t in range(3)]


def chunks():
    at = FIRST
    while at < LAST:
        size = min(CHUNK, LAST - at)
        yield at, size
        at += size


def newton(T, AX, AY, AZ, FZ, RES, RD, D):
    for it in range(NEWTON):
        for r, n in chunks():
            v = [T[ITER, t, r : r + n, :] for t in range(3)]
            k = [T[PERM, t, r : r + n, :] for t in range(3)]
            vy, ky = y_up(v), y_up(k)
            ay, fy, ax, fx = [], [], [], []
            for t in range(3):
                d = vy[t] - v[t]
                a = (0.5 * (ky[t] + k[t])) * g(d)
                AY[t, r : r + n, :] = a
                ay.append(a)
                fy.append(a * d)
                d = roll(v[t], -1, 1) - v[t]
                a = (0.5 * (roll(k[t], -1, 1) + k[t])) * g(d)
                AX[t, r : r + n, :] = a
                ax.append(a)
                fx.append(a * d)
            aym, fym = y_down(ay), y_down(fy)
            lane = iota((n, 128), 1)
            row = iota((n, 128), 0) + (r - FIRST)
            x, yl = lane % 16, lane // 16
            for t in range(3):
                d = T[ITER, t, r + 1 : r + n + 1, :] - v[t]
                az = (0.5 * (T[PERM, t, r + 1 : r + n + 1, :] + k[t])) * g(d)
                fz = az * d
                AZ[t, r : r + n, :] = az
                FZ[t, r : r + n, :] = fz
                azm = AZ[t, r - 1 : r + n - 1, :]
                fzm = FZ[t, r - 1 : r + n - 1, :]
                flow = (fz - fzm) + (fy[t] - fym[t]) + (fx[t] - roll(fx[t], 1, 1))
                weight = (az + azm) + (ay[t] + aym[t]) + (ax[t] + roll(ax[t], 1, 1))
                c = T[STORE, t, r : r + n, :]
                res = T[SRC, t, r : r + n, :] - c * v[t] + flow
                y = yl + 8 * t
                known = (x >= 1) & (x <= 14) & (y >= 1) & (y <= 22) & (row >= 1) & (row <= 134)
                rd = jnp.where(known, 1.0 / (c + weight), 0.0)
                RES[t, r : r + n, :] = res
                RD[t, r : r + n, :] = rd
                D[0, t, r : r + n, :] = res * rd
        for sweep in range(SWEEPS - 1):
            old, new = sweep % 2, (sweep + 1) % 2
            for r, n in chunks():
                d = [D[old, t, r : r + n, :] for t in range(3)]
                ay = [AY[t, r : r + n, :] for t in range(3)]
                up = y_up(d)
                down = y_down([ay[t] * d[t] for t in range(3)])
                for t in range(3):
                    ax = AX[t, r : r + n, :]
                    total = RES[t, r : r + n, :] + ay[t] * up[t] + down[t]
                    total += ax * roll(d[t], -1, 1) + roll(ax * d[t], 1, 1)
                    total += AZ[t, r : r + n, :] * D[old, t, r + 1 : r + n + 1, :]
                    total += AZ[t, r - 1 : r + n - 1, :] * D[old, t, r - 1 : r + n - 1, :]
                    delta = total * RD[t, r : r + n, :]
                    if sweep < SWEEPS - 2:
                        D[new, t, r : r + n, :] = delta
                    else:
                        T[ITER, t, r : r + n, :] = T[ITER, t, r : r + n, :] + delta


def coarse_flow(z, k, inv):
    n = len(z)
    flow, weight = [], []
    up = []
    for i in range(n):
        d = z[(i + 1) % n] - z[i]
        a = (0.5 * inv * inv * (k[(i + 1) % n] + k[i])) * g(d * inv)
        up.append((a, a * d))
    for i in range(n):
        a, f = up[i]
        am, fm = up[i - 1]
        w, fl = a + am, f - fm
        for axis in range(2):
            d = roll(z[i], -1, axis) - z[i]
            a = (0.5 * inv * inv * (roll(k[i], -1, axis) + k[i])) * g(d * inv)
            f = a * d
            w = w + (a + roll(a, 1, axis))
            fl = fl + (f - roll(f, 1, axis))
        flow.append(fl)
        weight.append(w)
    return flow, weight


def reaches(sizes):
    rx, ry, rz = (n // 2 for n in sizes)
    spare = max(rx - 1, 0) + max(ry - 1, 0) + max(rz - 1, 0)
    return spare <= 2 and 128 % (16 * sizes[2]) == 0


def kernel(
    sizes, it_ref, src_ref, perm_ref, store_ref, out,
    I, XR, XP, PR, PA, T, ZS, ZR, AX, AY, AZ, FZ, RES, RD, D, Q, CB, XS, XF, YF, FS, ZF,
    GS, GL, GA, GZ, GM, GY, GV, GX, CR,
    lsem, xs_sem, xr_sem, ys_sem, yr_sem, ps_sem, pr_sem, zs_sem, zr_sem, fs_sem, fr_sem, gs_sem, gr_sem,
):
    nx, ny, nz = sizes
    size = dict(zip(AXES, sizes))
    direct = reaches(sizes)
    me = {name: lax.axis_index(name) for name in AXES}

    def there(name, step):
        return {name: lax.rem(me[name] + (step + size[name]), size[name])}

    def send(src, dst, s, r, name, step):
        copy = pltpu.make_async_remote_copy(
            src_ref=src, dst_ref=dst, send_sem=s, recv_sem=r,
            device_id=there(name, step), device_id_type=pl.DeviceIdType.MESH,
        )
        copy.start()
        return copy

    barrier = pltpu.get_barrier_semaphore()
    greeted = [(name, step) for name in AXES for step in (1, -1)]
    if not direct:
        greeted = [(name, step) for name in AXES for step in range(1, size[name])]
    for name, step in greeted:
        pl.semaphore_signal(
            barrier, inc=1, device_id=there(name, step), device_id_type=pl.DeviceIdType.MESH
        )
    local = {}
    for a, ref in enumerate((it_ref, src_ref, perm_ref, store_ref)):
        local[a] = pltpu.make_async_copy(ref, I.at[a], lsem.at[a])
        local[a].start()
    for buf in (T,):
        for a in range(4):
            for t in range(3):
                buf[a, t, 0:FIRST, :] = jnp.zeros((FIRST, 128), F32)
                buf[a, t, LAST:ROWS, :] = jnp.zeros((ROWS - LAST, 128), F32)
    for buf in (AZ, FZ):
        for t in range(3):
            buf[t, 0:FIRST, :] = jnp.zeros((FIRST, 128), F32)
    for b in range(2):
        for t in range(3):
            D[b, t, 0:FIRST, :] = jnp.zeros((FIRST, 128), F32)
            D[b, t, LAST:ROWS, :] = jnp.zeros((ROWS - LAST, 128), F32)
    for a in range(4):
        local[a].wait()
    pl.semaphore_wait(barrier, len(greeted))

    sent = []
    xcopy, ycopy, zcopy = {}, {}, {}

    def fill_own(a):
        for x in range(8):
            PA[a, pl.ds(64 + 4 + x, 16, stride=16), :] = I[a, 16 * x : 16 * x + 16, :]

    def send_x(a, planes):
        n = 16 * planes
        hi = send(I.at[a, pl.ds(128 - n, n)], XR.at[a, 0, pl.ds(64 - n, n)], xs_sem.at[2 * a], xr_sem.at[2 * a], "gx", 1)
        lo = send(I.at[a, pl.ds(0, n)], XR.at[a, 1, pl.ds(0, n)], xs_sem.at[2 * a + 1], xr_sem.at[2 * a + 1], "gx", -1)
        xcopy[a] = (hi, lo)
        sent.extend([hi, lo])

    def fill_x(a, planes):
        for side in range(2):
            xcopy[a][side].wait_recv()
            for x in range(4 - planes, 4) if side == 0 else range(planes):
                PA[a, pl.ds(64 + 12 * side + x, 16, stride=16), :] = XR[a, side, 16 * x : 16 * x + 16, :]

    def send_y(a):
        hi = send(PA.at[a, pl.ds(256, 64)], PA.at[a, pl.ds(0, 64)], ys_sem.at[2 * a], yr_sem.at[2 * a], "gy", 1)
        lo = send(PA.at[a, pl.ds(64, 64)], PA.at[a, pl.ds(320, 64)], ys_sem.at[2 * a + 1], yr_sem.at[2 * a + 1], "gy", -1)
        ycopy[a] = (hi, lo)

    first, second = ORDER[:2], ORDER[2:]
    for a in first:
        send_x(a, 4)
    for a in second:
        fill_own(a)
        for x in (0, 15):
            PA[a, pl.ds(64 + x, 16, stride=16), :] = jnp.zeros((16, 128), F32)
        send_y(a)
    for a in second:
        send_x(a, 3)
    for a in first:
        fill_own(a)
    pieces = {}
    for n, a in enumerate(second):
        for copy in ycopy[a]:
            copy.wait_recv()
        for p in range(3):
            for side in range(2):
                x = (9, 4)[side] + p
                XP[n, side, 8 * p : 8 * p + 4, :] = PA[a, pl.ds(x, 4, stride=16), :]
                XP[n, side, 8 * p + 4 : 8 * p + 8, :] = PA[a, pl.ds(320 + x, 4, stride=16), :]
        pieces[a] = [
            send(XP.at[n, side], PR.at[n, side], ps_sem.at[2 * n + side], pr_sem.at[2 * n + side], "gx", (1, -1)[side])
            for side in range(2)
        ]
        sent.extend(pieces[a])
    for a in first:
        fill_x(a, 4)
        send_y(a)
        sent.extend(ycopy[a])

    def arrive(n, a):
        if a in first:
            for copy in ycopy[a]:
                copy.wait_recv()
            return
        for copy in ycopy[a]:
            copy.wait_send()
        fill_x(a, 3)
        for side in range(2):
            pieces[a][side].wait_recv()
            for p in range(3):
                x = (1, 12)[side] + p
                PA[a, pl.ds(x, 4, stride=16), :] = PR[n, side, 8 * p : 8 * p + 4, :]
                PA[a, pl.ds(320 + x, 4, stride=16), :] = PR[n, side, 8 * p + 4 : 8 * p + 8, :]
        for x in (0, 15):
            PA[a, pl.ds(x, 4, stride=16), :] = jnp.zeros((4, 128), F32)
            PA[a, pl.ds(320 + x, 4, stride=16), :] = jnp.zeros((4, 128), F32)

    for p in range(2):
        for h in range(2):
            a = ORDER[2 * p + h]
            arrive(h, a)
            for t in range(3):
                m = PA[a, 128 * t : 128 * t + 128, :].T
                T[a, t, 12:140, :] = m
                ZS[p, 0, t, 4 * h : 4 * h + 4, :] = m[124:128, :]
                ZS[p, 1, t, 4 * h : 4 * h + 4, :] = m[0:4, :]
        hi = send(ZS.at[p, 0], ZR.at[p, 0], zs_sem.at[2 * p], zr_sem.at[2 * p], "gz", 1)
        lo = send(ZS.at[p, 1], ZR.at[p, 1], zs_sem.at[2 * p + 1], zr_sem.at[2 * p + 1], "gz", -1)
        zcopy[p] = (hi, lo)
        sent += [hi, lo]
    for p in range(2):
        zcopy[p][0].wait_recv()
        zcopy[p][1].wait_recv()
        for h in range(2):
            a = ORDER[2 * p + h]
            for t in range(3):
                T[a, t, 8:12, :] = ZR[p, 0, t, 4 * h : 4 * h + 4, :]
                T[a, t, 140:144, :] = ZR[p, 1, t, 4 * h : 4 * h + 4, :]

    newton(T, AX, AY, AZ, FZ, RES, RD, D)

    for t in range(3):
        Q[128 * t : 128 * t + 128, :] = T[ITER, t, 12:140, :].T
    lane = iota((8, 128), 1)
    pack_c = jnp.zeros((8, 128), F32)
    pack_k = jnp.zeros((8, 128), F32)
    for y in range(16):
        b = (y + 4) * 16 + 4
        c = Q[b : b + 8, :]
        CB[8 * y : 8 * y + 8, :] = c
        pack_c = jnp.where(lane // 2 == y, roll(c, 1 + 2 * y, 1), pack_c)
        pack_k = jnp.where(lane // 2 == y, roll(PA[PERM, b : b + 8, :], 1 + 2 * y, 1), pack_k)
    XS[0, :, :] = Q[pl.ds(64 + 11, 16, stride=16), :]
    XS[1, :, :] = Q[pl.ds(64 + 4, 16, stride=16), :]
    FS[0:8, :] = pack_c
    FS[8:16, :] = pack_k
    faces = [
        send(XS.at[0], XF.at[0], fs_sem.at[0], fr_sem.at[0], "gx", 1),
        send(XS.at[1], XF.at[1], fs_sem.at[1], fr_sem.at[1], "gx", -1),
        send(CB.at[pl.ds(120, 8)], YF.at[0], fs_sem.at[2], fr_sem.at[2], "gy", 1),
        send(CB.at[pl.ds(0, 8)], YF.at[1], fs_sem.at[3], fr_sem.at[3], "gy", -1),
        send(FS, ZF.at[0], fs_sem.at[4], fr_sem.at[4], "gz", 1),
        send(FS, ZF.at[1], fs_sem.at[5], fr_sem.at[5], "gz", -1),
    ]
    sent += faces
    for copy in faces:
        copy.wait_recv()
    Q[pl.ds(64 + 3, 16, stride=16), :] = XF[0, :, :]
    Q[pl.ds(64 + 12, 16, stride=16), :] = XF[1, :, :]
    Q[3 * 16 + 4 : 3 * 16 + 12, :] = YF[0, :, :]
    Q[20 * 16 + 4 : 20 * 16 + 12, :] = YF[1, :, :]

    sums = [[None, None] for _ in range(4)]

    def add(q, j, value):
        sums[q][j] = value if sums[q][j] is None else sums[q][j] + value

    zf = [ZF[0, 0:8, :], ZF[1, 0:8, :]]
    zk = [ZF[0, 8:16, :], ZF[1, 8:16, :]]
    for y in range(16):
        b = (y + 4) * 16 + 4
        c, k = Q[b : b + 8, :], PA[PERM, b : b + 8, :]
        near = [(Q[b + o : b + o + 8, :], PA[PERM, b + o : b + o + 8, :]) for o in (1, -1, 16, -16)]
        near.append(tuple(
            jnp.where(lane == 127, roll(far, 126 - 2 * y, 1), roll(own, -1, 1))
            for far, own in ((zf[1], c), (zk[1], k))
        ))
        near.append(tuple(
            jnp.where(lane == 0, roll(far, -2 * y, 1), roll(own, 1, 1))
            for far, own in ((zf[0], c), (zk[0], k))
        ))
        flow = 0.0
        for cn, kn in near:
            d = cn - c
            flow = flow + (0.5 * (k + kn)) * g(d) * d
        st = PA[STORE, b : b + 8, :]
        j = y // 8
        add(0, j, c)
        add(1, j, PA[SRC, b : b + 8, :] - st * c + flow)
        add(2, j, k)
        add(3, j, st)
    rows = [jnp.sum(sums[q][j], axis=0, keepdims=True) for q in range(4) for j in range(2)]
    mean = jnp.where(iota((128, 128), 0) // 8 == iota((128, 128), 1) % 16, 1.0 / 512, 0.0).astype(F32)
    tile = jnp.dot(
        jnp.concatenate(rows, axis=0), mean,
        precision=lax.Precision.HIGHEST, preferred_element_type=F32,
    )

    width = GM.shape[-1]

    def gather(src, buf, name, base):
        n = size[name]
        copies = [
            send(src, buf.at[me[name]], gs_sem.at[base + s - 1], gr_sem.at[base + s - 1], name, s)
            for s in range(1, n)
        ]
        buf[me[name]] = src[...]
        for copy in copies:
            copy.wait_recv()
        sent.extend(copies)

    if direct:
        def at(i, j, k):
            return (i * ny + j) * nz + k

        own = iota((8, 128), 0) == iota((8, 128), 1) // 16
        GL[...] = jnp.sum(jnp.where(own, tile, 0.0), axis=0, keepdims=True)
        mine = at(*[me[name] for name in AXES])
        copies = []
        for i in range(nx):
            for j in range(ny):
                for k in range(nz):
                    if i + j + k:
                        copy = pltpu.make_async_remote_copy(
                            src_ref=GL, dst_ref=GA.at[mine],
                            send_sem=gs_sem.at[len(copies)], recv_sem=gr_sem.at[len(copies)],
                            device_id=tuple(
                                lax.rem(me[name] + step, size[name])
                                for name, step in zip(AXES, (i, j, k))
                            ),
                            device_id_type=pl.DeviceIdType.MESH,
                        )
                        copy.start()
                        copies.append(copy)
        GA[mine] = GL[...]
        for copy in copies:
            copy.wait_recv()
        sent.extend(copies)
        block = iota((8, 128), 0) == iota((8, 128), 1) // 16
        m, l = iota((128, 128), 0), iota((128, 128), 1)
        placed = 0.0
        for k in range(nz):
            lines = [
                jnp.where(block, jnp.broadcast_to(GA[at(i, j, k)], (8, 128)), 0.0)
                for i in range(nx) for j in range(ny)
            ]
            move = jnp.where((l // 16) % nz == k, jnp.where(l % 16 == m % 16, 1.0, 0.0), 0.0)
            placed = placed + jnp.dot(
                jnp.concatenate(lines, axis=0), move.astype(F32),
                precision=lax.Precision.HIGHEST, preferred_element_type=F32,
            )
        for i in range(nx):
            for j in range(ny):
                at_row = 8 * (i * ny + j)
                merged = placed[at_row : at_row + 8, :]
                for q in range(4):
                    GX[i, 8 * q + 2 * j : 8 * q + 2 * j + 2, :] = merged[2 * q : 2 * q + 2, :]
    else:
        GS[...] = tile
        gather(GS, GZ, "gz", 0)
        wlane = iota((8, width), 1)
        merged = None
        for z in range(nz):
            part = GZ[z]
            if width > 128:
                part = jnp.concatenate([part] * (width // 128), axis=1)
            merged = part if merged is None else jnp.where((wlane // 16) % nz == z, part, merged)
        GM[...] = merged
        gather(GM, GY, "gy", nz - 1)
        for y in range(ny):
            for q in range(4):
                GV[8 * q + 2 * y : 8 * q + 2 * y + 2, :] = GY[y, 2 * q : 2 * q + 2, :]
        gather(GV, GX, "gx", nz + ny - 2)

    base = [GX[i, 0:8, :] for i in range(nx)]
    cres = [GX[i, 8:16, :] for i in range(nx)]
    kc = [GX[i, 16:24, :] for i in range(nx)]
    sc = [GX[i, 24:32, :] for i in range(nx)]
    flow, weight = coarse_flow(base, kc, 1.0 / 8)
    rhs = [sc[i] * base[i] - flow[i] + cres[i] for i in range(nx)]
    z = [base[i] + cres[i] / (sc[i] + weight[i]) for i in range(nx)]
    for sweep in range(1, CSWEEPS):
        flow, weight = coarse_flow(z, kc, 1.0 / 8)
        z = [z[i] + (rhs[i] - sc[i] * z[i] + flow[i]) / (sc[i] + weight[i]) for i in range(nx)]
    for i in range(nx):
        CR[i, :, :] = z[i] - base[i]
    spread = jnp.where(
        iota((width, 128), 0) == 16 * me["gz"] + iota((width, 128), 1) // 8, 1.0, 0.0
    ).astype(F32)
    wide = jnp.dot(
        CR[me["gx"]], spread, precision=lax.Precision.HIGHEST, preferred_element_type=F32
    )
    sub = iota((8, 128), 0)
    for j in range(2):
        line = jnp.sum(jnp.where(sub == 2 * me["gy"] + j, wide, 0.0), axis=0, keepdims=True)
        for y in range(8 * j, 8 * j + 8):
            out[pl.ds(y, 8, stride=16), :] = CB[8 * y : 8 * y + 8, :] + line
    for copy in sent:
        copy.wait_send()


def shards(sizes, *args):
    nx, ny, nz = sizes
    width = max(128, 16 * nz)
    field = lambda *lead: pltpu.VMEM(lead + (3, ROWS, 128), F32)
    direct = reaches(sizes)
    links = nx * ny * nz - 1 if direct else nx + ny + nz - 3
    scratch = [
        pltpu.VMEM((4, 128, 128), F32),
        pltpu.VMEM((4, 2, 64, 128), F32),
        pltpu.VMEM((2, 2, 24, 128), F32),
        pltpu.VMEM((2, 2, 24, 128), F32),
        pltpu.VMEM((4, 384, 128), F32),
        field(4),
        pltpu.VMEM((2, 2, 3, 8, 128), F32),
        pltpu.VMEM((2, 2, 3, 8, 128), F32),
        field(), field(), field(), field(), field(), field(), field(2),
        pltpu.VMEM((384, 128), F32),
        pltpu.VMEM((128, 128), F32),
        pltpu.VMEM((2, 16, 128), F32),
        pltpu.VMEM((2, 16, 128), F32),
        pltpu.VMEM((2, 8, 128), F32),
        pltpu.VMEM((16, 128), F32),
        pltpu.VMEM((2, 16, 128), F32),
        pltpu.VMEM((8, 128), F32),
        pltpu.VMEM((1, 128), F32),
        pltpu.VMEM((nx * ny * nz if direct else 1, 1, 128), F32),
        pltpu.VMEM((nz, 8, 128), F32),
        pltpu.VMEM((8, width), F32),
        pltpu.VMEM((ny, 8, width), F32),
        pltpu.VMEM((32, width), F32),
        pltpu.VMEM((nx, 32, width), F32),
        pltpu.VMEM((nx, 8, width), F32),
    ] + [pltpu.SemaphoreType.DMA((n,)) for n in (4, 8, 8, 8, 8, 4, 4, 4, 4, 6, 6, links, links)]
    out = pl.pallas_call(
        functools.partial(kernel, sizes),
        out_shape=jax.ShapeDtypeStruct((128, 128), F32),
        in_specs=[pl.BlockSpec(memory_space=pl.ANY)] * 4,
        out_specs=pl.BlockSpec(memory_space=pltpu.VMEM),
        scratch_shapes=scratch,
        compiler_params=pltpu.CompilerParams(
            collective_id=0, has_side_effects=True, vmem_limit_bytes=60 * 1024 * 1024
        ),
    )(*[x.reshape(128, 128) for x in args])
    return out.reshape(8, 16, 128)


def solution(mesh):
    spec = P(*AXES)
    sizes = tuple(mesh.shape[name] for name in AXES)
    return jax.shard_map(
        functools.partial(shards, sizes), mesh=mesh, in_specs=(spec,) * 4, out_specs=spec, check_vma=False
    )
```
